32 devices in a mesh: dp: 4 (over z), seq: 8 (over y, x, core).
Axes of the slice: x: 2, y: 2, z: 4, core: 2. Of those that a mesh axis runs over, the one named last changes fastest.
Arguments:
- hidden: bfloat16 [4, 2048, 1024], P('dp', 'seq'), may hold values from -6 to 6
- segment_ids: int32 [4, 2048], P('dp'), may hold values from 0 to 31, never falling along the last dimension, each value on 1 to 512 neighbouring positions
- kernel: float32 [31, 1024], replicated, may hold values from -1 to 1
- norm_gain: float32 [1024], replicated, may hold values from 0.5 to 1.5
- projection: bfloat16 [1024, 1024], replicated, may hold values from -0.1875 to 0.1875
- cotangent: bfloat16 [4, 2048, 1024], P('dp', 'seq'), may hold values from -6 to 6
Outputs:
- conv_out: bfloat16 [4, 2048, 1024], P('dp', 'seq')
- grad_hidden: bfloat16 [4, 2048, 1024], P('dp', 'seq')
- grad_projection: float32 [1024, 1024], P('seq')
- grad_kernel: float32 [1024, 31], P('seq')
- grad_gain: float32 [1024], P('seq')
The draws below stay inside these ranges and needn't reach their ends.
Inputs may be any that keep to these rules, and one draw needn't show every extreme that they name: `segment_ids`: within a row utterance numbers never fall, every number 0 to 31 occurs, each utterance spans 1 to 512 frames and one spans exactly 512.
All inputs are finite; a program needn't handle non-finite values.
Results may differ from the reference program's by a relative error of at most 0.005.
Values may be sent and summed in bfloat16 or wider, within the bound.
A program may use at most 64 MiB of HBM per device.

```python
import math
import jax
import jax.numpy as jnp
import numpy as np
from jax import lax

D = 1024
KERNEL = 31
FRAMES = 2048
UTTS = 32
SPAN = 512
N_DP = 4


def spiked(result, stream_key, source, target, parts, factor):
    def block_of(position):
        return (jnp.arange(result.shape[position]) // (result.shape[position] // parts)).reshape((-1,) + (1,) * (result.ndim - 1 - position))

    near = jax.random.permutation(stream_key, parts)[block_of(target)]
    other_side = (block_of(target) + parts // 2) % parts
    return jnp.where((block_of(source) == near) | (block_of(source) == other_side), factor * result, result)


def levels(key, dims, cuts, least, high):
    def one(position, parts):
        draws = jax.random.uniform(jax.random.fold_in(jax.random.fold_in(key, 6), position), (parts,), jnp.float32, least / len(cuts), high / len(cuts))
        return jnp.repeat(jnp.exp(draws), dims[position] // parts).reshape((-1,) + (1,) * (len(dims) - position - 1))

    factor_of = one(*cuts[0])
    for cut in cuts[1:]:
        factor_of = factor_of * one(*cut)
    return factor_of


def profile(amount, total, most, skew):
    portions = [(1 << 20) // math.isqrt(grade ** skew) + 1 for grade in range(2, amount + 1)]
    rest, given = total - most - (amount - 1), [1] * (amount - 1)
    while rest > 0:
        free = [i for i in range(amount - 1) if given[i] < most]
        pool, budget = sum([portions[i] for i in free]), rest
        for i in free:
            extra = min(most - given[i], max(1, budget * portions[i] // pool), rest)
            given[i] = given[i] + extra
            rest = rest - extra
    return np.array([most] + given)


def ragged(stream_key, amount, total, most, skew):
    if amount == 2:
        one = jax.random.randint(stream_key, (), max(1, total - most), min(most, total - 1) + 1)
        return jnp.stack([one, total - one])
    sizes = jnp.asarray(profile(amount, total, most, skew), jnp.int32)
    couples = (amount - 1) // 2
    giver, sink = sizes[1:1 + 2 * couples:2], sizes[2:2 + 2 * couples:2]
    room = jnp.minimum(giver - 1, most - sink)
    passed = jax.random.randint(jax.random.fold_in(stream_key, 1), (couples,), 0, 1 << 20) % (room + 1)
    sizes = sizes.at[1:1 + 2 * couples:2].set(giver - passed).at[2:2 + 2 * couples:2].set(sink + passed)
    return sizes[jax.random.permutation(jax.random.fold_in(stream_key, 2), amount)]


def noise(stream_key, dims, spread, most, cuts=(), held_as=jnp.bfloat16):
    entries = jax.random.normal(stream_key, dims, jnp.float32) * spread
    if len(cuts) > 0:
        entries = levels(stream_key, dims, cuts, -0.22, 0.18) * entries
    return jnp.clip(entries, min=-most, max=most).astype(held_as)


def gaussian_with(stream_key, shape, scale, limit, shards, heavy, kind=jnp.bfloat16):
    result = scale * jax.random.normal(stream_key, shape, jnp.float32)
    if shards:
        result = result * levels(stream_key, shape, shards, -0.22, 0.18)
    return jnp.clip(spiked(result, jax.random.fold_in(stream_key, 3), *heavy), -limit, limit).astype(kind)


def setup_inputs(seed: int = 0) -> dict:
    key_of = jax.random.split(jax.random.key(seed), 7)
    hidden = noise(key_of[0], (N_DP, FRAMES, D), 1.0, 6.0, ((0, 4), (1, 8)))
    segment_ids = jax.vmap(lambda own: jnp.searchsorted(jnp.cumsum(ragged(own, UTTS, FRAMES, SPAN, 2)), jnp.arange(FRAMES), side="right"))(jax.random.split(key_of[1], N_DP)).reshape((N_DP, FRAMES)).astype(jnp.int32)
    kernel = noise(key_of[2], (KERNEL, D), KERNEL ** -0.5, 1.0, (), jnp.float32)
    norm_gain = jnp.clip(1.0 + 0.1 * jax.random.normal(key_of[3], (D,), jnp.float32), 0.5, 1.5)
    projection = noise(key_of[4], (D, D), D ** -0.5, 0.1875)
    cotangent = gaussian_with(key_of[5], (N_DP, FRAMES, D), 1.0, 6.0, ((0, 4), (1, 8)), (1, 2, 8, 2.0))
    return dict(hidden=hidden, segment_ids=segment_ids, kernel=kernel, norm_gain=norm_gain, projection=projection, cotangent=cotangent)


EPS = 1e-05

def depth_forward(padded, segs, kernel, length):
    reach = KERNEL // 2
    total = jnp.zeros((length, kernel.shape[1]), jnp.float32)
    centre = segs[reach:reach + length]
    for offset in range(KERNEL):
        same = (segs[offset:offset + length] == centre).astype(jnp.float32)[:, None]
        total = total + kernel[offset] * padded[offset:offset + length].astype(jnp.float32) * same
    return total

def kernel_terms(grad, padded, segs, length):
    reach = KERNEL // 2
    centre = segs[reach:reach + length]
    rows_out = []
    for offset in range(KERNEL):
        same = (segs[offset:offset + length] == centre).astype(jnp.float32)[:, None]
        rows_out.append(lax.optimization_barrier(jnp.sum(grad * padded[offset:offset + length].astype(jnp.float32) * same, 0)))
    return jnp.stack(rows_out, 0)

def spread_back(grid, segs, kernel, length):
    reach = KERNEL // 2
    total = jnp.zeros((length, kernel.shape[1]), jnp.float32)
    centre = segs[reach:reach + length]
    for offset in range(KERNEL):
        lower = 2 * reach - offset
        same = (segs[lower:lower + length] == centre).astype(jnp.float32)[:, None]
        total = total + kernel[offset] * grid[lower:lower + length] * same
    return total

def norm_forward(mixed, norm_gain):
    centred = mixed - lax.optimization_barrier(jnp.mean(mixed, -1, keepdims=True))
    variance = lax.optimization_barrier(jnp.mean(centred * centred, -1, keepdims=True))
    scale_inv = lax.rsqrt(variance + EPS)
    normed = centred * scale_inv
    gated = normed * norm_gain
    sigma = jax.nn.sigmoid(gated)
    act = (gated * sigma).astype(jnp.bfloat16)
    return (normed, scale_inv, gated, sigma, act)

def norm_backward(grad_act, normed, scale_inv, gated, sigma, norm_gain):
    grad_gated = grad_act * sigma * (1.0 + gated * (1.0 - sigma))
    grad_normed = grad_gated * norm_gain
    grad_mixed = scale_inv * (grad_normed - lax.optimization_barrier(jnp.mean(grad_normed, -1, keepdims=True)) - normed * lax.optimization_barrier(jnp.mean(grad_normed * normed, -1, keepdims=True)))
    return (grad_gated, grad_mixed)

def reference(hidden, segment_ids, kernel, norm_gain, projection, cotangent):
    reach = KERNEL // 2

    def one_row(items):
        frames_row, seg_row, grad_out = items
        padded_in = jnp.pad(frames_row, ((reach, reach), (0, 0)))
        seg_pad = jnp.pad(seg_row, reach, constant_values=-1)
        mixed = depth_forward(padded_in, seg_pad, kernel, FRAMES)
        normed, scale_inv, gated, sigma, act = norm_forward(mixed, norm_gain)
        conv_out = jnp.dot(act, projection.T, preferred_element_type=jnp.float32).astype(jnp.bfloat16)
        grad_act = jnp.dot(grad_out, projection, preferred_element_type=jnp.float32)
        grad_gated, grad_mixed = norm_backward(grad_act, normed, scale_inv, gated, sigma, norm_gain)
        kernel_grad = kernel_terms(grad_mixed, padded_in, seg_pad, FRAMES)
        gain_grad = lax.optimization_barrier(jnp.sum(grad_gated * normed, 0))
        grad_padded = jnp.pad(grad_mixed, ((reach, reach), (0, 0)))
        grad_frames = spread_back(grad_padded, seg_pad, kernel, FRAMES).astype(jnp.bfloat16)
        weight_grad = jnp.dot(grad_out.T, act, preferred_element_type=jnp.float32)
        return (conv_out, grad_frames, weight_grad, kernel_grad, gain_grad)
    conv_out, grad_hidden, weight_grad, kernel_grad, gain_grad = lax.map(one_row, (hidden, segment_ids, cotangent))
    factor = 1.0 / math.sqrt(FRAMES * N_DP)
    grad_projection = lax.optimization_barrier(jnp.sum(weight_grad, 0)) * factor
    grad_kernel = lax.optimization_barrier(jnp.sum(kernel_grad, 0)).T * factor
    grad_gain = lax.optimization_barrier(jnp.sum(gain_grad, 0)) * factor
    return (conv_out, grad_hidden, grad_projection, grad_kernel, grad_gain)
```

```python
import functools
import math

import jax
import jax.numpy as jnp
from jax import lax
from jax.experimental import pallas as pl
from jax.experimental.pallas import tpu as pltpu
from jax.sharding import PartitionSpec as P

EPS = 1e-05
LANES = 128
SUB = 8
CHUNK = 16
HALO = 32
EDGE = 16
MESH = pl.DeviceIdType.MESH
F32 = jnp.float32
BF16 = jnp.bfloat16


def row_mean(parts, width):
    total = parts[0]
    for part in parts[1:]:
        total = total + part
    return jnp.sum(total, axis=1, keepdims=True) * (1.0 / width)


def local_kernel(
    seg, hid, before, after, kern, gain, proj, cot,
    conv_out, grad_hidden, shares,
    mask, frames, cot_ext, cot_t, taps_b, grad_act, normed, sigma, inv, act, grad_mixed, gain_acc, small,
):
    length, width = hid.shape
    taps = kern.shape[0]
    reach = taps // 2
    slabs = width // LANES
    ext = length + 2 * EDGE
    cols = lambda s: pl.ds(s * LANES, LANES)

    for s in range(slabs):
        frames[s, :HALO, :] = before[:HALO, cols(s)].astype(F32)
        frames[s, HALO : HALO + length, :] = hid[:, cols(s)].astype(F32)
        frames[s, HALO + length :, :] = after[:HALO, cols(s)].astype(F32)
        for k in range(taps):
            taps_b[s, k] = jnp.broadcast_to(kern[k : k + 1, cols(s)], (SUB, LANES))
    cot_ext[:EDGE, :] = before[HALO:, :]
    cot_ext[EDGE : EDGE + length, :] = cot[...]
    cot_ext[EDGE + length :, :] = after[HALO:, :]
    cot_t[...] = cot[...].T
    gain_acc[...] = jnp.zeros_like(gain_acc)
    small[...] = jnp.zeros_like(small)

    @pl.loop(0, ext // SUB)
    def _(i):
        row = pl.multiple_of(i * SUB, SUB)
        own = seg[pl.ds(row + EDGE, SUB), :]
        for k in range(taps):
            there = seg[pl.ds(row + EDGE - reach + k, SUB), :]
            mask[k, pl.ds(row, SUB), :] = (there == own).astype(F32)

    @pl.loop(0, ext // CHUNK)
    def _(i):
        base = pl.multiple_of(i * CHUNK, CHUNK)
        tiles = CHUNK // SUB
        acc = [[jnp.zeros((SUB, LANES), F32) for _ in range(slabs)] for _ in range(tiles)]
        for k in range(taps):
            same = [mask[k, pl.ds(base + SUB * t, SUB), :] for t in range(tiles)]
            for s in range(slabs):
                tap = taps_b[s, k]
                for t in range(tiles):
                    there = frames[s, pl.ds(base + SUB * t + EDGE - reach + k, SUB), :]
                    acc[t][s] = acc[t][s] + tap * (there * same[t])
        acts = [[None] * slabs for _ in range(tiles)]
        for t in range(tiles):
            rows = pl.ds(base + SUB * t, SUB)
            mean = row_mean(acc[t], width)
            centred = [a - mean for a in acc[t]]
            var = row_mean([c * c for c in centred], width)
            scale = lax.rsqrt(var + EPS)
            inv[rows, :] = jnp.broadcast_to(scale, (SUB, LANES))
            for s in range(slabs):
                n = centred[s] * scale
                gated = n * gain[:, cols(s)]
                sig = jax.nn.sigmoid(gated)
                normed[rows, cols(s)] = n
                sigma[rows, cols(s)] = sig
                acts[t][s] = gated * sig
        for s in range(slabs):
            act[pl.ds(base, CHUNK), cols(s)] = jnp.concatenate([a[s] for a in acts], 0).astype(BF16)

    block = 256
    dims = lambda a, b: (((a,), (b,)), ((), ()))

    @pl.loop(0, width // block)
    def _(j):
        span = pl.ds(pl.multiple_of(j * block, block), block)
        shares[:, span] = lax.dot_general(
            cot_t[...], act[EDGE : EDGE + length, span], dims(1, 0), preferred_element_type=F32
        ).astype(BF16)
        grad_act[:, span] = lax.dot_general(
            cot_ext[...], proj[:, span], dims(1, 0), preferred_element_type=F32
        )
        conv_out[:, span] = lax.dot_general(
            act[EDGE : EDGE + length, :], proj[span, :], dims(1, 1), preferred_element_type=F32
        ).astype(BF16)

    @pl.loop(0, ext // SUB)
    def _(i):
        base = pl.multiple_of(i * SUB, SUB)
        rows = pl.ds(base, SUB)
        inside = jnp.logical_and(i >= EDGE // SUB, i < (EDGE + length) // SUB).astype(F32)
        ns, gns = [], []
        for s in range(slabs):
            n = normed[rows, cols(s)]
            sig = sigma[rows, cols(s)]
            g = gain[:, cols(s)]
            gg = grad_act[rows, cols(s)] * sig * (1.0 + n * g * (1.0 - sig))
            gain_acc[s] += inside * (gg * n)
            ns.append(n)
            gns.append(gg * g)
        m1 = row_mean(gns, width)
        m2 = row_mean([a * b for a, b in zip(gns, ns)], width)
        scale = inv[rows, :]
        for s in range(slabs):
            grad_mixed[s, rows, :] = scale * (gns[s] - m1 - ns[s] * m2)

    @pl.loop(0, slabs)
    def _(s):
        lanes = pl.ds(pl.multiple_of(s * LANES, LANES), LANES)

        def step(i, sums):
            base = pl.multiple_of(i * CHUNK, CHUNK)
            tiles = CHUNK // SUB
            sums = list(sums)
            outs = [jnp.zeros((SUB, LANES), F32) for _ in range(tiles)]
            here = [frames[s, pl.ds(base + HALO + SUB * t, SUB), :] for t in range(tiles)]
            for k in range(taps):
                back = taps - 1 - k
                tap = taps_b[s, k]
                for t in range(tiles):
                    row = base + EDGE + SUB * t
                    part = grad_mixed[s, pl.ds(row - reach + back, SUB), :] * mask[back, pl.ds(row, SUB), :]
                    outs[t] = outs[t] + tap * part
                    sums[k] = sums[k] + here[t] * part
            grad_hidden[pl.ds(base, CHUNK), lanes] = jnp.concatenate(outs, 0).astype(BF16)
            return tuple(sums)

        zeros = tuple(jnp.zeros((SUB, LANES), F32) for _ in range(taps))
        sums = lax.fori_loop(0, length // CHUNK, step, zeros)
        for k in range(taps):
            small[k : k + 1, :] = jnp.sum(sums[k], axis=0, keepdims=True)
        small[taps : taps + 1, :] = jnp.sum(gain_acc[s], axis=0, keepdims=True)
        shares[lanes, width:] = small[...].T.astype(BF16)


def local_part(seg, hid, before, after, kern, gain, proj, cot):
    length, width = hid.shape
    taps = kern.shape[0]
    slabs = width // LANES
    ext = length + 2 * EDGE
    vmem = pl.BlockSpec(memory_space=pltpu.VMEM)
    return pl.pallas_call(
        local_kernel,
        out_shape=(
            jax.ShapeDtypeStruct((length, width), BF16),
            jax.ShapeDtypeStruct((length, width), BF16),
            jax.ShapeDtypeStruct((width, width + LANES), BF16),
        ),
        in_specs=[vmem] * 8,
        out_specs=(vmem,) * 3,
        scratch_shapes=[
            pltpu.VMEM((taps, ext, LANES), F32),
            pltpu.VMEM((slabs, length + 2 * HALO, LANES), F32),
            pltpu.VMEM((ext, width), BF16),
            pltpu.VMEM((width, length), BF16),
            pltpu.VMEM((slabs, taps, SUB, LANES), F32),
            pltpu.VMEM((ext, width), F32),
            pltpu.VMEM((ext, width), F32),
            pltpu.VMEM((ext, width), F32),
            pltpu.VMEM((ext, LANES), F32),
            pltpu.VMEM((ext, width), BF16),
            pltpu.VMEM((slabs, ext, LANES), F32),
            pltpu.VMEM((slabs, SUB, LANES), F32),
            pltpu.VMEM((LANES, LANES), F32),
        ],
        compiler_params=pltpu.CompilerParams(vmem_limit_bytes=40 << 20),
        name="local_part",
    )(seg, hid, before, after, kern, gain, proj, cot)


def sum_kernel(
    n_dp, n_seq, factor,
    shares, out, tail,
    mate_in, chip_out, chip_in, total, dp_out, dp_in, gather,
    a_send, a_recv, b_send, b_recv, c_send, c_recv, d_send, d_recv,
):
    dp, seq = lax.axis_index("dp"), lax.axis_index("seq")
    chips = n_seq // 2
    chip, core = seq // 2, lax.rem(seq, 2)
    mate = chip * 2 + (1 - core)
    rows, width = total.shape
    wide = out.shape[1]
    split = dp_in.shape[1] != rows
    sub = dp_in.shape[1]

    barrier = pltpu.get_barrier_semaphore()
    pl.semaphore_signal(barrier, inc=1, device_id=(dp, mate), device_id_type=MESH)
    for d in range(1, chips):
        to = lax.rem(chip + d, chips) * 2 + core
        pl.semaphore_signal(barrier, inc=1, device_id=(dp, to), device_id_type=MESH)
    for d in range(1, n_dp):
        to = lax.rem(dp + d, n_dp)
        pl.semaphore_signal(barrier, inc=1, device_id=(to, seq), device_id_type=MESH)
    pl.semaphore_wait(barrier, 1 + (chips - 1) + (n_dp - 1))

    def block_of(c, k):
        return shares.at[pl.ds(pl.multiple_of((c * 2 + k) * rows, rows), rows), :]

    def to_mate(d):
        c = lax.rem(chip + d, chips)
        return pltpu.make_async_remote_copy(
            src_ref=block_of(c, 1 - core), dst_ref=mate_in.at[d],
            send_sem=a_send.at[d], recv_sem=a_recv.at[d],
            device_id=(dp, mate), device_id_type=MESH,
        )

    def to_chip(d):
        return pltpu.make_async_remote_copy(
            src_ref=chip_out.at[d], dst_ref=chip_in.at[d],
            send_sem=b_send.at[d], recv_sem=b_recv.at[d],
            device_id=(dp, lax.rem(chip + d, chips) * 2 + core), device_id_type=MESH,
        )

    order = list(range(1, chips)) + [0]
    for d in order:
        to_mate(d).start()
    for d in order:
        to_mate(d).wait_recv()
        c = lax.rem(chip + d, chips)
        pair = block_of(c, core)[...].astype(F32) + mate_in[d].astype(F32)
        if d:
            chip_out[d] = pair.astype(BF16)
            to_chip(d).start()
        else:
            total[...] = pair
    for d in range(1, chips):
        to_chip(d).wait_recv()
        total[...] += chip_in[d].astype(F32)

    def place(p):
        return pl.ds(pl.multiple_of(p * sub, sub), sub) if split else pl.ds(0, rows)

    dp_out[...] = total[...].astype(BF16)

    def to_group(d):
        to = lax.rem(dp + d, n_dp)
        return pltpu.make_async_remote_copy(
            src_ref=dp_out.at[place(to), :], dst_ref=dp_in.at[dp],
            send_sem=c_send.at[d], recv_sem=c_recv.at[d],
            device_id=(to, seq), device_id_type=MESH,
        )

    def from_group(d):
        at = lax.rem(dp - d + n_dp, n_dp)
        return pltpu.make_async_remote_copy(
            src_ref=dp_out.at[place(at), :], dst_ref=dp_in.at[at],
            send_sem=c_send.at[d], recv_sem=c_recv.at[d],
            device_id=(at, seq), device_id_type=MESH,
        )

    for d in range(1, n_dp):
        to_group(d).start()
    dp_in[dp] = dp_out[place(dp), :]
    for d in range(1, n_dp):
        from_group(d).wait_recv()
    done = dp_in[0].astype(F32)
    for p in range(1, n_dp):
        done = done + dp_in[p].astype(F32)
    done = done * factor
    if split:
        gather[place(dp), :] = done.astype(BF16)

        def to_all(d):
            return pltpu.make_async_remote_copy(
                src_ref=gather.at[place(dp), :], dst_ref=gather.at[place(dp), :],
                send_sem=d_send.at[d], recv_sem=d_recv.at[d],
                device_id=(lax.rem(dp + d, n_dp), seq), device_id_type=MESH,
            )

        def from_all(d):
            at = lax.rem(dp - d + n_dp, n_dp)
            return pltpu.make_async_remote_copy(
                src_ref=gather.at[place(at), :], dst_ref=gather.at[place(at), :],
                send_sem=d_send.at[d], recv_sem=d_recv.at[d],
                device_id=(at, seq), device_id_type=MESH,
            )

        for d in range(1, n_dp):
            to_all(d).start()
        for d in range(1, n_dp):
            from_all(d).wait_recv()
        out[...] = gather[:, :wide].astype(F32)
        tail[...] = gather[:, wide:].astype(F32)
        for d in range(1, n_dp):
            to_all(d).wait_send()
    else:
        out[...] = done[:, :wide]
        tail[...] = done[:, wide:]
    for d in order:
        to_mate(d).wait_send()
        if d:
            to_chip(d).wait_send()
    for d in range(1, n_dp):
        to_group(d).wait_send()


def sum_part(shares, n_dp, n_seq, factor):
    width = shares.shape[0]
    cols = shares.shape[1]
    rows = width // n_seq
    chips = n_seq // 2
    split = rows % (16 * n_dp) == 0
    sub = rows // n_dp if split else rows
    vmem = pl.BlockSpec(memory_space=pltpu.VMEM)
    sem = lambda n: pltpu.SemaphoreType.DMA((n,))
    return pl.pallas_call(
        functools.partial(sum_kernel, n_dp, n_seq, factor),
        out_shape=(
            jax.ShapeDtypeStruct((rows, width), F32),
            jax.ShapeDtypeStruct((rows, cols - width), F32),
        ),
        in_specs=[vmem],
        out_specs=(vmem, vmem),
        scratch_shapes=[
            pltpu.VMEM((chips, rows, cols), BF16),
            pltpu.VMEM((chips, rows, cols), BF16),
            pltpu.VMEM((chips, rows, cols), BF16),
            pltpu.VMEM((rows, cols), F32),
            pltpu.VMEM((rows, cols), BF16),
            pltpu.VMEM((n_dp, sub, cols), BF16),
            pltpu.VMEM((rows, cols), BF16),
            sem(chips), sem(chips), sem(chips), sem(chips),
            sem(n_dp), sem(n_dp), sem(n_dp), sem(n_dp),
        ],
        compiler_params=pltpu.CompilerParams(
            collective_id=0, has_side_effects=True, vmem_limit_bytes=24 << 20
        ),
        name="sum_part",
    )(shares)


def body(n_dp, n_seq, hidden, segment_ids, kernel, norm_gain, projection, cotangent):
    hid, cot = hidden[0], cotangent[0]
    length, width = hid.shape
    taps = kernel.shape[0]
    start = lax.axis_index("seq") * length
    seg_row = jnp.pad(segment_ids[0], HALO, constant_values=-1)
    seg_wide = lax.dynamic_slice_in_dim(seg_row, start, length + 2 * HALO)
    seg = jnp.broadcast_to(seg_wide[:, None], (length + 2 * HALO, LANES))
    up = [(i, i + 1) for i in range(n_seq - 1)]
    down = [(j, i) for i, j in up]
    before = lax.ppermute(jnp.concatenate([hid[length - HALO :], cot[length - EDGE :]], 0), "seq", up)
    after = lax.ppermute(jnp.concatenate([hid[:HALO], cot[:EDGE]], 0), "seq", down)
    gain = jnp.broadcast_to(norm_gain[None, :], (SUB, width))
    conv_out, grad_hidden, shares = local_part(seg, hid, before, after, kernel, gain, projection, cot)
    factor = 1.0 / math.sqrt(length * n_seq * n_dp)
    weight, tail = sum_part(shares, n_dp, n_seq, factor)
    return (conv_out[None], grad_hidden[None], weight, tail[:, :taps], tail[:, taps])


def solution(mesh):
    n_dp, n_seq = mesh.shape["dp"], mesh.shape["seq"]
    in_specs = (P("dp", "seq", None), P("dp", None), P(), P(), P(), P("dp", "seq", None))
    out_specs = (
        P("dp", "seq", None),
        P("dp", "seq", None),
        P("seq", None),
        P("seq", None),
        P("seq"),
    )
    return jax.shard_map(
        functools.partial(body, n_dp, n_seq), mesh=mesh, in_specs=in_specs, out_specs=out_specs, check_vma=False
    )
```

```python
import functools
import math

import jax
import jax.numpy as jnp
from jax import lax
from jax.experimental import pallas as pl
from jax.experimental.pallas import tpu as pltpu
from jax.sharding import PartitionSpec as P

EPS = 1e-05
LANES = 128
SUB = 8
CHUNK = 16
HALO = 32
EDGE = 16
MESH = pl.DeviceIdType.MESH
F32 = jnp.float32
BF16 = jnp.bfloat16


def row_mean(parts, width):
    total = parts[0]
    for part in parts[1:]:
        total = total + part
    return jnp.sum(total, axis=1, keepdims=True) * (1.0 / width)


def fused_kernel(
    n_dp, n_seq, factor,
    seg, kern, gain, hid, proj_in, cot,
    conv_out, grad_hidden, out, tail,
    mask, frames, hid_v, proj, edge_b, edge_a, cot_ext, cot_t, taps_b, grad_act, normed, sigma, inv, act,
    grad_mixed, gain_acc, small, turn, shares, mate_in, chip_out, chip_in, total, dp_out, dp_in, gather,
    small_in, small_sum, small_dp,
    l_sem, h_send, h_recv, a_send, a_recv, b_send, b_recv, c_send, c_recv, d_send, d_recv,
    e_send, e_recv, f_send, f_recv,
):
    length, width = hid.shape
    taps = kern.shape[0]
    reach = taps // 2
    slabs = width // LANES
    ext = length + 2 * EDGE
    inner = pl.ds(EDGE, length)
    cols = lambda s: pl.ds(s * LANES, LANES)
    dims = lambda a, b: (((a,), (b,)), ((), ()))

    dp, seq = lax.axis_index("dp"), lax.axis_index("seq")
    chips = n_seq // 2
    chip, core = seq // 2, lax.rem(seq, 2)
    mate = chip * 2 + (1 - core)
    right, left = lax.rem(seq + 1, n_seq), lax.rem(seq + n_seq - 1, n_seq)
    rows = out.shape[0]
    sub = dp_in.shape[1]
    split = sub != rows

    loads = [
        pltpu.make_async_copy(hid, hid_v, l_sem.at[0]),
        pltpu.make_async_copy(cot, cot_ext.at[inner, :], l_sem.at[1]),
        pltpu.make_async_copy(proj_in, proj, l_sem.at[2]),
    ]
    for load in loads:
        load.start()

    barrier = pltpu.get_barrier_semaphore()
    for d in range(1, n_seq):
        to = lax.rem(seq + d, n_seq)
        pl.semaphore_signal(barrier, inc=1, device_id=(dp, to), device_id_type=MESH)
    for d in range(1, n_dp):
        to = lax.rem(dp + d, n_dp)
        pl.semaphore_signal(barrier, inc=1, device_id=(to, seq), device_id_type=MESH)

    def remote(src, dst, send, recv, device):
        return pltpu.make_async_remote_copy(
            src_ref=src, dst_ref=dst, send_sem=send, recv_sem=recv, device_id=device, device_id_type=MESH
        )

    @pl.loop(0, ext // SUB)
    def _(i):
        row = pl.multiple_of(i * SUB, SUB)
        own = seg[pl.ds(row + EDGE, SUB), :]
        for k in range(taps):
            there = seg[pl.ds(row + EDGE - reach + k, SUB), :]
            mask[k, pl.ds(row, SUB), :] = (there == own).astype(F32)

    pl.semaphore_wait(barrier, (n_seq - 1) + (n_dp - 1))

    def edge_copies():
        return [
            remote(hid.at[pl.ds(length - HALO, HALO), :], edge_b, h_send.at[0], h_recv.at[0], (dp, right)),
            remote(hid.at[pl.ds(0, HALO), :], edge_a, h_send.at[1], h_recv.at[1], (dp, left)),
            remote(cot.at[pl.ds(length - EDGE, EDGE), :], cot_ext.at[pl.ds(0, EDGE), :],
                   h_send.at[2], h_recv.at[2], (dp, right)),
            remote(cot.at[pl.ds(0, EDGE), :], cot_ext.at[pl.ds(EDGE + length, EDGE), :],
                   h_send.at[3], h_recv.at[3], (dp, left)),
        ]

    edges = edge_copies()
    for copy in edges:
        copy.start()

    for s in range(slabs):
        for k in range(taps):
            taps_b[s, k] = jnp.broadcast_to(kern[k : k + 1, cols(s)], (SUB, LANES))
    gain_acc[...] = jnp.zeros_like(gain_acc)
    turn[...] = jnp.zeros_like(turn)
    loads[0].wait()
    for s in range(slabs):
        frames[s, HALO : HALO + length, :] = hid_v[:, cols(s)].astype(F32)
    loads[1].wait()
    cot_t[...] = cot_ext[inner, :].T

    def forward(i):
        base = pl.multiple_of(i * CHUNK, CHUNK)
        tiles = CHUNK // SUB
        acc = [[jnp.zeros((SUB, LANES), F32) for _ in range(slabs)] for _ in range(tiles)]
        for k in range(taps):
            same = [mask[k, pl.ds(base + SUB * t, SUB), :] for t in range(tiles)]
            for s in range(slabs):
                tap = taps_b[s, k]
                for t in range(tiles):
                    there = frames[s, pl.ds(base + SUB * t + EDGE - reach + k, SUB), :]
                    acc[t][s] = acc[t][s] + tap * (there * same[t])
        acts = [[None] * slabs for _ in range(tiles)]
        for t in range(tiles):
            at = pl.ds(base + SUB * t, SUB)
            mean = row_mean(acc[t], width)
            centred = [a - mean for a in acc[t]]
            var = row_mean([c * c for c in centred], width)
            scale = lax.rsqrt(var + EPS)
            inv[at, :] = jnp.broadcast_to(scale, (SUB, LANES))
            for s in range(slabs):
                n = centred[s] * scale
                gated = n * gain[:, cols(s)]
                sig = jax.nn.sigmoid(gated)
                normed[at, cols(s)] = n
                sigma[at, cols(s)] = sig
                acts[t][s] = gated * sig
        for s in range(slabs):
            act[pl.ds(base, CHUNK), cols(s)] = jnp.concatenate([a[s] for a in acts], 0).astype(BF16)

    count = ext // CHUNK

    @pl.loop(2, count - 2)
    def _(i):
        forward(i)

    edges[0].wait_recv()
    edges[1].wait_recv()
    for s in range(slabs):
        frames[s, :HALO, :] = edge_b[:, cols(s)].astype(F32)
        frames[s, HALO + length :, :] = edge_a[:, cols(s)].astype(F32)

    @pl.loop(0, 4)
    def _(i):
        forward(i + (i // 2) * (count - 4))

    def block_dot(c, k):
        at = pl.ds(pl.multiple_of((c * 2 + k) * rows, rows), rows)
        return lax.dot_general(cot_t[at, :], act[inner, :], dims(1, 0), preferred_element_type=F32)

    def to_mate(d):
        return remote(shares.at[d], mate_in.at[d], a_send.at[d], a_recv.at[d], (dp, mate))

    def to_chip(d):
        to = lax.rem(chip + d, chips) * 2 + core
        return remote(chip_out.at[d], chip_in.at[d], b_send.at[d], b_recv.at[d], (dp, to))

    order = list(range(1, chips)) + [0]
    for d in order:
        shares[d] = block_dot(lax.rem(chip + d, chips), 1 - core).astype(BF16)
        to_mate(d).start()

    for d in order:
        pair = block_dot(lax.rem(chip + d, chips), core)
        to_mate(d).wait_recv()
        pair = pair + mate_in[d].astype(F32)
        if d:
            chip_out[d] = pair.astype(BF16)
            to_chip(d).start()
        else:
            total[...] = pair

    loads[2].wait()
    edges[2].wait_recv()
    edges[3].wait_recv()
    block = 256

    @pl.loop(0, width // block)
    def _(j):
        span = pl.ds(pl.multiple_of(j * block, block), block)
        grad_act[:, span] = lax.dot_general(
            cot_ext[...], proj[:, span], dims(1, 0), preferred_element_type=F32
        )
        conv_out[:, span] = lax.dot_general(
            act[inner, :], proj[span, :], dims(1, 1), preferred_element_type=F32
        ).astype(BF16)

    @pl.loop(0, ext // SUB)
    def _(i):
        at = pl.ds(pl.multiple_of(i * SUB, SUB), SUB)
        inside = jnp.logical_and(i >= EDGE // SUB, i < (EDGE + length) // SUB).astype(F32)
        ns, gns = [], []
        for s in range(slabs):
            n = normed[at, cols(s)]
            sig = sigma[at, cols(s)]
            g = gain[:, cols(s)]
            gg = grad_act[at, cols(s)] * sig * (1.0 + n * g * (1.0 - sig))
            gain_acc[s] += inside * (gg * n)
            ns.append(n)
            gns.append(gg * g)
        m1 = row_mean(gns, width)
        m2 = row_mean([a * b for a, b in zip(gns, ns)], width)
        scale = inv[at, :]
        for s in range(slabs):
            grad_mixed[s, at, :] = scale * (gns[s] - m1 - ns[s] * m2)

    def slab_grads(s):
        lanes = pl.ds(pl.multiple_of(s * LANES, LANES), LANES)

        def step(i, sums):
            base = pl.multiple_of(i * CHUNK, CHUNK)
            tiles = CHUNK // SUB
            sums = list(sums)
            outs = [jnp.zeros((SUB, LANES), F32) for _ in range(tiles)]
            here = [frames[s, pl.ds(base + HALO + SUB * t, SUB), :] for t in range(tiles)]
            for k in range(taps):
                back = taps - 1 - k
                tap = taps_b[s, k]
                for t in range(tiles):
                    row = base + EDGE + SUB * t
                    part = grad_mixed[s, pl.ds(row - reach + back, SUB), :] * mask[back, pl.ds(row, SUB), :]
                    outs[t] = outs[t] + tap * part
                    sums[k] = sums[k] + here[t] * part
            grad_hidden[pl.ds(base, CHUNK), lanes] = jnp.concatenate(outs, 0).astype(BF16)
            return tuple(sums)

        zeros = tuple(jnp.zeros((SUB, LANES), F32) for _ in range(taps))
        sums = lax.fori_loop(0, length // CHUNK, step, zeros)
        for k in range(taps):
            small[s, k : k + 1, :] = jnp.sum(sums[k], axis=0, keepdims=True)
        small[s, taps : taps + 1, :] = jnp.sum(gain_acc[s], axis=0, keepdims=True)

    half = slabs // 2

    @pl.loop(0, half)
    def _(s):
        slab_grads(s)

    def place(p):
        return pl.ds(pl.multiple_of(p * sub, sub), sub) if split else pl.ds(0, rows)

    def group_at(d):
        return lax.rem(dp + d, n_dp), lax.rem(dp - d + n_dp, n_dp)

    def group_copy(d, slot, to):
        return remote(dp_out.at[place(to), :], dp_in.at[slot], c_send.at[d], c_recv.at[d], (to, seq))

    for d in range(1, chips):
        to_chip(d).wait_recv()
        total[...] += chip_in[d].astype(F32)
    dp_out[...] = total[...].astype(BF16)
    for d in range(1, n_dp):
        group_copy(d, dp, group_at(d)[0]).start()
    dp_in[dp] = dp_out[place(dp), :]

    @pl.loop(half, slabs)
    def _(s):
        slab_grads(s)

    def my_slab(j):
        return (j * rows) // LANES

    def small_copy(d, to):
        return remote(small.at[my_slab(to)], small_in.at[d], e_send.at[d], e_recv.at[d], (dp, to))

    for d in range(1, n_seq):
        small_copy(d, lax.rem(seq + d, n_seq)).start()

    for d in range(1, n_dp):
        group_copy(d, group_at(d)[1], group_at(d)[1]).wait_recv()
    done = dp_in[0].astype(F32)
    for p in range(1, n_dp):
        done = done + dp_in[p].astype(F32)
    done = done * factor

    def gather_copy(d, p, to):
        return remote(gather.at[place(p), :], gather.at[place(p), :], d_send.at[d], d_recv.at[d], (to, seq))

    if split:
        gather[place(dp), :] = done.astype(BF16)
        for d in range(1, n_dp):
            gather_copy(d, dp, group_at(d)[0]).start()
    else:
        out[...] = done

    mine = small[my_slab(seq)]
    for d in range(1, n_seq):
        small_copy(d, lax.rem(seq + d, n_seq)).wait_recv()
        mine = mine + small_in[d]
    small_sum[...] = mine

    def tail_copy(d, slot, to):
        return remote(small_sum, small_dp.at[slot], f_send.at[d], f_recv.at[d], (to, seq))

    for d in range(1, n_dp):
        tail_copy(d, dp, group_at(d)[0]).start()
    small_dp[dp] = mine

    if split:
        for d in range(1, n_dp):
            gather_copy(d, group_at(d)[1], group_at(d)[1]).wait_recv()
        out[...] = gather[...].astype(F32)

    for d in range(1, n_dp):
        tail_copy(d, group_at(d)[1], group_at(d)[1]).wait_recv()
    whole = small_dp[0]
    for p in range(1, n_dp):
        whole = whole + small_dp[p]
    turn[: taps + 1, :] = whole * factor
    turn[...] = turn[...].T
    tail[...] = turn[pl.ds(pl.multiple_of(lax.rem(seq * rows, LANES), min(rows, LANES)), rows), :]

    for copy in edges:
        copy.wait_send()
    for d in order:
        to_mate(d).wait_send()
        if d:
            to_chip(d).wait_send()
    for d in range(1, n_seq):
        small_copy(d, lax.rem(seq + d, n_seq)).wait_send()
    for d in range(1, n_dp):
        group_copy(d, dp, group_at(d)[0]).wait_send()
        tail_copy(d, dp, group_at(d)[0]).wait_send()
        if split:
            gather_copy(d, dp, group_at(d)[0]).wait_send()


def fused(seg, kern, gain, hid, proj, cot, n_dp, n_seq, factor):
    length, width = hid.shape
    taps = kern.shape[0]
    slabs = width // LANES
    ext = length + 2 * EDGE
    rows = width // n_seq
    chips = n_seq // 2
    split = rows % (16 * n_dp) == 0
    sub = rows // n_dp if split else rows
    vmem = pl.BlockSpec(memory_space=pltpu.VMEM)
    hbm = pl.BlockSpec(memory_space=pl.ANY)
    sem = lambda n: pltpu.SemaphoreType.DMA((n,))
    return pl.pallas_call(
        functools.partial(fused_kernel, n_dp, n_seq, factor),
        out_shape=(
            jax.ShapeDtypeStruct((length, width), BF16),
            jax.ShapeDtypeStruct((length, width), BF16),
            jax.ShapeDtypeStruct((rows, width), F32),
            jax.ShapeDtypeStruct((rows, LANES), F32),
        ),
        in_specs=[vmem] * 3 + [hbm] * 3,
        out_specs=(vmem,) * 4,
        scratch_shapes=[
            pltpu.VMEM((taps, ext, LANES), F32),
            pltpu.VMEM((slabs, length + 2 * HALO, LANES), F32),
            pltpu.VMEM((length, width), BF16),
            pltpu.VMEM((width, width), BF16),
            pltpu.VMEM((HALO, width), BF16),
            pltpu.VMEM((HALO, width), BF16),
            pltpu.VMEM((ext, width), BF16),
            pltpu.VMEM((width, length), BF16),
            pltpu.VMEM((slabs, taps, SUB, LANES), F32),
            pltpu.VMEM((ext, width), F32),
            pltpu.VMEM((ext, width), F32),
            pltpu.VMEM((ext, width), F32),
            pltpu.VMEM((ext, LANES), F32),
            pltpu.VMEM((ext, width), BF16),
            pltpu.VMEM((slabs, ext, LANES), F32),
            pltpu.VMEM((slabs, SUB, LANES), F32),
            pltpu.VMEM((slabs, taps + 1, LANES), F32),
            pltpu.VMEM((LANES, LANES), F32),
            pltpu.VMEM((chips, rows, width), BF16),
            pltpu.VMEM((chips, rows, width), BF16),
            pltpu.VMEM((chips, rows, width), BF16),
            pltpu.VMEM((chips, rows, width), BF16),
            pltpu.VMEM((rows, width), F32),
            pltpu.VMEM((rows, width), BF16),
            pltpu.VMEM((n_dp, sub, width), BF16),
            pltpu.VMEM((rows, width), BF16),
            pltpu.VMEM((n_seq, taps + 1, LANES), F32),
            pltpu.VMEM((taps + 1, LANES), F32),
            pltpu.VMEM((n_dp, taps + 1, LANES), F32),
            sem(3), sem(4), sem(4), sem(chips), sem(chips), sem(chips), sem(chips),
            sem(n_dp), sem(n_dp), sem(n_dp), sem(n_dp), sem(n_seq), sem(n_seq), sem(n_dp), sem(n_dp),
        ],
        compiler_params=pltpu.CompilerParams(
            collective_id=0, has_side_effects=True, vmem_limit_bytes=48 << 20
        ),
        name="fused",
    )(seg, kern, gain, hid, proj, cot)


def body(n_dp, n_seq, hidden, segment_ids, kernel, norm_gain, projection, cotangent):
    hid, cot = hidden[0], cotangent[0]
    length, width = hid.shape
    taps = kernel.shape[0]
    start = lax.axis_index("seq") * length
    seg_row = jnp.pad(segment_ids[0], HALO, constant_values=-1)
    seg_wide = lax.dynamic_slice_in_dim(seg_row, start, length + 2 * HALO)
    seg = jnp.broadcast_to(seg_wide[:, None], (length + 2 * HALO, LANES))
    gain = norm_gain[None, :]
    factor = 1.0 / math.sqrt(length * n_seq * n_dp)
    conv_out, grad_hidden, weight, tail = fused(
        seg, kernel, gain, hid, projection, cot, n_dp, n_seq, factor
    )
    return (conv_out[None], grad_hidden[None], weight, tail[:, :taps], tail[:, taps])


def solution(mesh):
    n_dp, n_seq = mesh.shape["dp"], mesh.shape["seq"]
    in_specs = (P("dp", "seq", None), P("dp", None), P(), P(), P(), P("dp", "seq", None))
    out_specs = (
        P("dp", "seq", None),
        P("dp", "seq", None),
        P("seq", None),
        P("seq", None),
        P("seq"),
    )
    return jax.shard_map(
        functools.partial(body, n_dp, n_seq), mesh=mesh, in_specs=in_specs, out_specs=out_specs, check_vma=False
    )
```

```python
import functools
import math

import jax
import jax.numpy as jnp
from jax import lax
from jax.experimental import pallas as pl
from jax.experimental.pallas import tpu as pltpu
from jax.sharding import PartitionSpec as P

EPS = 1e-05
LANES = 128
SUB = 8
CHUNK = 16
HALO = 32
EDGE = 16
MESH = pl.DeviceIdType.MESH
F32 = jnp.float32
BF16 = jnp.bfloat16


def row_mean(parts, width):
    total = parts[0]
    for part in parts[1:]:
        total = total + part
    return jnp.sum(total, axis=1, keepdims=True) * (1.0 / width)


def fused_kernel(
    n_dp, n_seq, factor,
    seg, kern_in, gain_in, hid, proj_in, cot,
    conv_to, hidden_to, out, tail,
    kern, gain, conv_out, grad_hidden,
    mask, frames, hid_v, proj, edge_b, edge_a, cot_ext, cot_t, taps_b, grad_act, normed, sigma, inv, act,
    grad_mixed, gain_acc, small, turn, shares, mate_in, chip_out, chip_in, total, dp_out, dp_in, gather,
    small_in, small_sum, small_dp,
    l_sem, h_send, h_recv, a_send, a_recv, b_send, b_recv, c_send, c_recv, d_send, d_recv,
    e_send, e_recv, f_send, f_recv,
):
    length, width = hid.shape
    taps = kern.shape[0]
    reach = taps // 2
    slabs = width // LANES
    ext = length + 2 * EDGE
    inner = pl.ds(EDGE, length)
    cols = lambda s: pl.ds(s * LANES, LANES)
    dims = lambda a, b: (((a,), (b,)), ((), ()))

    dp, seq = lax.axis_index("dp"), lax.axis_index("seq")
    chips = n_seq // 2
    chip, core = seq // 2, lax.rem(seq, 2)
    mate = chip * 2 + (1 - core)
    right, left = lax.rem(seq + 1, n_seq), lax.rem(seq + n_seq - 1, n_seq)
    rows = out.shape[0]
    sub = dp_in.shape[2]
    parts = shares.shape[0]
    part = width // parts
    piece = lambda h: pl.ds(h * part, part)
    split = sub != rows

    loads = [
        pltpu.make_async_copy(hid, hid_v, l_sem.at[0]),
        pltpu.make_async_copy(cot, cot_ext.at[inner, :], l_sem.at[1]),
        pltpu.make_async_copy(proj_in, proj, l_sem.at[2]),
        pltpu.make_async_copy(kern_in, kern, l_sem.at[3]),
        pltpu.make_async_copy(gain_in, gain, l_sem.at[4]),
    ]
    conv_store = pltpu.make_async_copy(conv_out, conv_to, l_sem.at[5])
    hidden_store = pltpu.make_async_copy(grad_hidden, hidden_to, l_sem.at[6])
    for load in loads:
        load.start()

    barrier = pltpu.get_barrier_semaphore()
    for d in range(1, n_seq):
        to = lax.rem(seq + d, n_seq)
        pl.semaphore_signal(barrier, inc=1, device_id=(dp, to), device_id_type=MESH)
    for d in range(1, n_dp):
        to = lax.rem(dp + d, n_dp)
        pl.semaphore_signal(barrier, inc=1, device_id=(to, seq), device_id_type=MESH)

    def remote(src, dst, send, recv, device):
        return pltpu.make_async_remote_copy(
            src_ref=src, dst_ref=dst, send_sem=send, recv_sem=recv, device_id=device, device_id_type=MESH
        )

    @pl.loop(0, ext // SUB)
    def _(i):
        row = pl.multiple_of(i * SUB, SUB)
        own = seg[pl.ds(row + EDGE, SUB), :]
        for k in range(taps):
            there = seg[pl.ds(row + EDGE - reach + k, SUB), :]
            mask[k, pl.ds(row, SUB), :] = (there == own).astype(F32)

    pl.semaphore_wait(barrier, (n_seq - 1) + (n_dp - 1))

    def edge_copies():
        return [
            remote(hid.at[pl.ds(length - HALO, HALO), :], edge_b, h_send.at[0], h_recv.at[0], (dp, right)),
            remote(hid.at[pl.ds(0, HALO), :], edge_a, h_send.at[1], h_recv.at[1], (dp, left)),
            remote(cot.at[pl.ds(length - EDGE, EDGE), :], cot_ext.at[pl.ds(0, EDGE), :],
                   h_send.at[2], h_recv.at[2], (dp, right)),
            remote(cot.at[pl.ds(0, EDGE), :], cot_ext.at[pl.ds(EDGE + length, EDGE), :],
                   h_send.at[3], h_recv.at[3], (dp, left)),
        ]

    edges = edge_copies()
    for copy in edges:
        copy.start()

    loads[3].wait()
    loads[4].wait()
    for s in range(slabs):
        for k in range(taps):
            taps_b[s, k] = jnp.broadcast_to(kern[k : k + 1, cols(s)], (SUB, LANES))
    gain_acc[...] = jnp.zeros_like(gain_acc)
    turn[...] = jnp.zeros_like(turn)
    loads[0].wait()
    for s in range(slabs):
        frames[s, HALO : HALO + length, :] = hid_v[:, cols(s)].astype(F32)
    loads[1].wait()
    cot_t[...] = cot_ext[inner, :].T

    def forward(i):
        base = pl.multiple_of(i * CHUNK, CHUNK)
        tiles = CHUNK // SUB
        acc = [[jnp.zeros((SUB, LANES), F32) for _ in range(slabs)] for _ in range(tiles)]
        for k in range(taps):
            same = [mask[k, pl.ds(base + SUB * t, SUB), :] for t in range(tiles)]
            for s in range(slabs):
                tap = taps_b[s, k]
                for t in range(tiles):
                    there = frames[s, pl.ds(base + SUB * t + EDGE - reach + k, SUB), :]
                    acc[t][s] = acc[t][s] + tap * (there * same[t])
        acts = [[None] * slabs for _ in range(tiles)]
        for t in range(tiles):
            at = pl.ds(base + SUB * t, SUB)
            mean = row_mean(acc[t], width)
            centred = [a - mean for a in acc[t]]
            var = row_mean([c * c for c in centred], width)
            scale = lax.rsqrt(var + EPS)
            inv[at, :] = jnp.broadcast_to(scale, (SUB, LANES))
            for s in range(slabs):
                n = centred[s] * scale
                gated = n * gain[:, cols(s)]
                sig = jax.nn.sigmoid(gated)
                normed[at, cols(s)] = n
                sigma[at, cols(s)] = sig
                acts[t][s] = gated * sig
        for s in range(slabs):
            act[pl.ds(base, CHUNK), cols(s)] = jnp.concatenate([a[s] for a in acts], 0).astype(BF16)

    count = ext // CHUNK

    @pl.loop(2, count - 2)
    def _(i):
        forward(i)

    edges[0].wait_recv()
    edges[1].wait_recv()
    for s in range(slabs):
        frames[s, :HALO, :] = edge_b[:, cols(s)].astype(F32)
        frames[s, HALO + length :, :] = edge_a[:, cols(s)].astype(F32)

    @pl.loop(0, 2)
    def _(i):
        forward(1 + i * (count - 3))

    def block_dot(h, c, k):
        at = pl.ds(pl.multiple_of((c * 2 + k) * rows, rows), rows)
        return lax.dot_general(cot_t[at, :], act[inner, piece(h)], dims(1, 0), preferred_element_type=F32)

    def to_mate(h, d):
        return remote(shares.at[h, d], mate_in.at[h, d], a_send.at[h, d], a_recv.at[h, d], (dp, mate))

    def to_chip(h, d):
        to = lax.rem(chip + d, chips) * 2 + core
        return remote(chip_out.at[h, d], chip_in.at[h, d], b_send.at[h, d], b_recv.at[h, d], (dp, to))

    order = list(range(1, chips)) + [0]
    for h in range(parts):
        for d in order:
            shares[h, d] = block_dot(h, lax.rem(chip + d, chips), 1 - core).astype(BF16)
            to_mate(h, d).start()

    for h in range(parts):
        for d in order:
            pair = block_dot(h, lax.rem(chip + d, chips), core)
            to_mate(h, d).wait_recv()
            pair = pair + mate_in[h, d].astype(F32)
            if d:
                chip_out[h, d] = pair.astype(BF16)
                to_chip(h, d).start()
            else:
                total[:, piece(h)] = pair

    @pl.loop(0, 2)
    def _(i):
        forward(i * (count - 1))

    loads[2].wait()
    edges[2].wait_recv()
    edges[3].wait_recv()
    block = 256

    @pl.loop(0, width // block)
    def _(j):
        span = pl.ds(pl.multiple_of(j * block, block), block)
        grad_act[:, span] = lax.dot_general(
            cot_ext[...], proj[:, span], dims(1, 0), preferred_element_type=F32
        )
        conv_out[:, span] = lax.dot_general(
            act[inner, :], proj[span, :], dims(1, 1), preferred_element_type=F32
        ).astype(BF16)

    conv_store.start()

    @pl.loop(0, ext // SUB)
    def _(i):
        at = pl.ds(pl.multiple_of(i * SUB, SUB), SUB)
        inside = jnp.logical_and(i >= EDGE // SUB, i < (EDGE + length) // SUB).astype(F32)
        ns, gns = [], []
        for s in range(slabs):
            n = normed[at, cols(s)]
            sig = sigma[at, cols(s)]
            g = gain[:, cols(s)]
            gg = grad_act[at, cols(s)] * sig * (1.0 + n * g * (1.0 - sig))
            gain_acc[s] += inside * (gg * n)
            ns.append(n)
            gns.append(gg * g)
        m1 = row_mean(gns, width)
        m2 = row_mean([a * b for a, b in zip(gns, ns)], width)
        scale = inv[at, :]
        for s in range(slabs):
            grad_mixed[s, at, :] = scale * (gns[s] - m1 - ns[s] * m2)

    def slab_grads(s):
        lanes = pl.ds(pl.multiple_of(s * LANES, LANES), LANES)

        def step(i, sums):
            base = pl.multiple_of(i * CHUNK, CHUNK)
            tiles = CHUNK // SUB
            sums = list(sums)
            outs = [jnp.zeros((SUB, LANES), F32) for _ in range(tiles)]
            here = [frames[s, pl.ds(base + HALO + SUB * t, SUB), :] for t in range(tiles)]
            for k in range(taps):
                back = taps - 1 - k
                tap = taps_b[s, k]
                for t in range(tiles):
                    row = base + EDGE + SUB * t
                    part = grad_mixed[s, pl.ds(row - reach + back, SUB), :] * mask[back, pl.ds(row, SUB), :]
                    outs[t] = outs[t] + tap * part
                    sums[k] = sums[k] + here[t] * part
            grad_hidden[pl.ds(base, CHUNK), lanes] = jnp.concatenate(outs, 0).astype(BF16)
            return tuple(sums)

        zeros = tuple(jnp.zeros((SUB, LANES), F32) for _ in range(taps))
        sums = lax.fori_loop(0, length // CHUNK, step, zeros)
        for k in range(taps):
            small[s, k : k + 1, :] = jnp.sum(sums[k], axis=0, keepdims=True)
        small[s, taps : taps + 1, :] = jnp.sum(gain_acc[s], axis=0, keepdims=True)

    def place(p):
        return pl.ds(pl.multiple_of(p * sub, sub), sub) if split else pl.ds(0, rows)

    def group_at(d):
        return lax.rem(dp + d, n_dp), lax.rem(dp - d + n_dp, n_dp)

    def group_copy(h, d, slot, to):
        return remote(
            dp_out.at[h, place(to), :], dp_in.at[h, slot], c_send.at[h, d], c_recv.at[h, d], (to, seq)
        )

    def gather_copy(h, d, p, to):
        return remote(
            gather.at[h, place(p), :], gather.at[h, place(p), :], d_send.at[h, d], d_recv.at[h, d], (to, seq)
        )

    def sum_chips(h):
        own = total[:, piece(h)]
        for d in range(1, chips):
            to_chip(h, d).wait_recv()
            own = own + chip_in[h, d].astype(F32)
        dp_out[h] = own.astype(BF16)
        for d in range(1, n_dp):
            group_copy(h, d, dp, group_at(d)[0]).start()
        dp_in[h, dp] = dp_out[h, place(dp), :]

    def sum_groups(h):
        for d in range(1, n_dp):
            group_copy(h, d, group_at(d)[1], group_at(d)[1]).wait_recv()
        done = dp_in[h, 0].astype(F32)
        for p in range(1, n_dp):
            done = done + dp_in[h, p].astype(F32)
        done = done * factor
        if split:
            gather[h, place(dp), :] = done.astype(BF16)
            for d in range(1, n_dp):
                gather_copy(h, d, dp, group_at(d)[0]).start()
        else:
            out[:, piece(h)] = done

    def slabs_between(first, last):
        @pl.loop(first, last)
        def _(s):
            slab_grads(s)

    quarter = slabs // 4
    sum_chips(0)
    slabs_between(0, 2 * quarter)
    sum_chips(1)
    sum_groups(0)
    slabs_between(2 * quarter, 3 * quarter)
    sum_groups(1)
    slabs_between(3 * quarter, slabs)

    def my_slab(j):
        return (j * rows) // LANES

    def small_copy(d, to):
        return remote(small.at[my_slab(to)], small_in.at[d], e_send.at[d], e_recv.at[d], (dp, to))

    for d in range(1, n_seq):
        small_copy(d, lax.rem(seq + d, n_seq)).start()
    hidden_store.start()

    mine = small[my_slab(seq)]
    for d in range(1, n_seq):
        small_copy(d, lax.rem(seq + d, n_seq)).wait_recv()
        mine = mine + small_in[d]
    small_sum[...] = mine

    def tail_copy(d, slot, to):
        return remote(small_sum, small_dp.at[slot], f_send.at[d], f_recv.at[d], (to, seq))

    for d in range(1, n_dp):
        tail_copy(d, dp, group_at(d)[0]).start()
    small_dp[dp] = mine

    if split:
        for h in range(parts):
            for d in range(1, n_dp):
                gather_copy(h, d, group_at(d)[1], group_at(d)[1]).wait_recv()
            out[:, piece(h)] = gather[h].astype(F32)

    for d in range(1, n_dp):
        tail_copy(d, group_at(d)[1], group_at(d)[1]).wait_recv()
    whole = small_dp[0]
    for p in range(1, n_dp):
        whole = whole + small_dp[p]
    turn[: taps + 1, :] = whole * factor
    turn[...] = turn[...].T
    tail[...] = turn[pl.ds(pl.multiple_of(lax.rem(seq * rows, LANES), min(rows, LANES)), rows), :]

    for copy in edges:
        copy.wait_send()
    for h in range(parts):
        for d in order:
            to_mate(h, d).wait_send()
            if d:
                to_chip(h, d).wait_send()
        for d in range(1, n_dp):
            group_copy(h, d, dp, group_at(d)[0]).wait_send()
            if split:
                gather_copy(h, d, dp, group_at(d)[0]).wait_send()
    for d in range(1, n_seq):
        small_copy(d, lax.rem(seq + d, n_seq)).wait_send()
    for d in range(1, n_dp):
        tail_copy(d, dp, group_at(d)[0]).wait_send()
    conv_store.wait()
    hidden_store.wait()


def fused(seg, kern, gain, hid, proj, cot, n_dp, n_seq, factor):
    length, width = hid.shape
    taps = kern.shape[0]
    slabs = width // LANES
    ext = length + 2 * EDGE
    rows = width // n_seq
    chips = n_seq // 2
    split = rows % (16 * n_dp) == 0
    sub = rows // n_dp if split else rows
    vmem = pl.BlockSpec(memory_space=pltpu.VMEM)
    hbm = pl.BlockSpec(memory_space=pl.ANY)
    parts = 2
    part = width // parts
    sem = lambda *n: pltpu.SemaphoreType.DMA(n)
    return pl.pallas_call(
        functools.partial(fused_kernel, n_dp, n_seq, factor),
        out_shape=(
            jax.ShapeDtypeStruct((length, width), BF16),
            jax.ShapeDtypeStruct((length, width), BF16),
            jax.ShapeDtypeStruct((rows, width), F32),
            jax.ShapeDtypeStruct((rows, LANES), F32),
        ),
        in_specs=[vmem] + [hbm] * 5,
        out_specs=(hbm, hbm, vmem, vmem),
        scratch_shapes=[
            pltpu.VMEM((taps, width), F32),
            pltpu.VMEM((1, width), F32),
            pltpu.VMEM((length, width), BF16),
            pltpu.VMEM((length, width), BF16),
            pltpu.VMEM((taps, ext, LANES), F32),
            pltpu.VMEM((slabs, length + 2 * HALO, LANES), F32),
            pltpu.VMEM((length, width), BF16),
            pltpu.VMEM((width, width), BF16),
            pltpu.VMEM((HALO, width), BF16),
            pltpu.VMEM((HALO, width), BF16),
            pltpu.VMEM((ext, width), BF16),
            pltpu.VMEM((width, length), BF16),
            pltpu.VMEM((slabs, taps, SUB, LANES), F32),
            pltpu.VMEM((ext, width), F32),
            pltpu.VMEM((ext, width), F32),
            pltpu.VMEM((ext, width), F32),
            pltpu.VMEM((ext, LANES), F32),
            pltpu.VMEM((ext, width), BF16),
            pltpu.VMEM((slabs, ext, LANES), F32),
            pltpu.VMEM((slabs, SUB, LANES), F32),
            pltpu.VMEM((slabs, taps + 1, LANES), F32),
            pltpu.VMEM((LANES, LANES), F32),
            pltpu.VMEM((parts, chips, rows, part), BF16),
            pltpu.VMEM((parts, chips, rows, part), BF16),
            pltpu.VMEM((parts, chips, rows, part), BF16),
            pltpu.VMEM((parts, chips, rows, part), BF16),
            pltpu.VMEM((rows, width), F32),
            pltpu.VMEM((parts, rows, part), BF16),
            pltpu.VMEM((parts, n_dp, sub, part), BF16),
            pltpu.VMEM((parts, rows, part), BF16),
            pltpu.VMEM((n_seq, taps + 1, LANES), F32),
            pltpu.VMEM((taps + 1, LANES), F32),
            pltpu.VMEM((n_dp, taps + 1, LANES), F32),
            sem(7), sem(4), sem(4),
            sem(parts, chips), sem(parts, chips), sem(parts, chips), sem(parts, chips),
            sem(parts, n_dp), sem(parts, n_dp), sem(parts, n_dp), sem(parts, n_dp),
            sem(n_seq), sem(n_seq), sem(n_dp), sem(n_dp),
        ],
        compiler_params=pltpu.CompilerParams(
            collective_id=0, has_side_effects=True, vmem_limit_bytes=60 << 20
        ),
        name="fused",
    )(seg, kern, gain, hid, proj, cot)


def body(n_dp, n_seq, hidden, segment_ids, kernel, norm_gain, projection, cotangent):
    hid, cot = hidden[0], cotangent[0]
    length, width = hid.shape
    taps = kernel.shape[0]
    start = lax.axis_index("seq") * length
    seg_row = jnp.pad(segment_ids[0], HALO, constant_values=-1)
    seg_wide = lax.dynamic_slice_in_dim(seg_row, start, length + 2 * HALO)
    seg = jnp.broadcast_to(seg_wide[:, None], (length + 2 * HALO, LANES))
    gain = norm_gain[None, :]
    factor = 1.0 / math.sqrt(length * n_seq * n_dp)
    conv_out, grad_hidden, weight, tail = fused(
        seg, kernel, gain, hid, projection, cot, n_dp, n_seq, factor
    )
    return (conv_out[None], grad_hidden[None], weight, tail[:, :taps], tail[:, taps])


def solution(mesh):
    n_dp, n_seq = mesh.shape["dp"], mesh.shape["seq"]
    in_specs = (P("dp", "seq", None), P("dp", None), P(), P(), P(), P("dp", "seq", None))
    out_specs = (
        P("dp", "seq", None),
        P("dp", "seq", None),
        P("seq", None),
        P("seq", None),
        P("seq"),
    )
    return jax.shard_map(
        functools.partial(body, n_dp, n_seq), mesh=mesh, in_specs=in_specs, out_specs=out_specs, check_vma=False
    )
```
